256 devices in a mesh: dom: 64 (over z, y, core), rows: 4 (over x).
Axes of the slice: x: 4, y: 4, z: 8, core: 2. Of those that a mesh axis runs over, the one named last changes fastest.
Arguments:
- images: bfloat16 [28672, 25600], P('dom', 'rows'), may hold values from -6 to 6
- panels: bfloat16 [128, 25600, 256], P('dom', 'rows')
- mean_panels: float32 [128, 25600], P('dom', 'rows'), may hold values from -6 to 6
- ctf_table: float32 [16, 25600], P(None, 'rows'), may hold values from -1 to 1
- pose_bin: int32 [28672], P('dom'), may hold values from 0 to 1
- ctf_group: int32 [28672], P('dom'), may hold values from 0 to 15
Outputs:
- scores: float32 [28672, 256], P('dom')
- factor: float32 [256, 256], replicated
The draws below stay inside these ranges and needn't reach their ends.
All inputs are finite; a program needn't handle non-finite values.
Results may differ from the reference program's by a relative error of at most 0.003.
Values sent between devices are 32-bit elements; how exact they have to be, the bound alone decides.
No kernel may reach another device: no remote copies, remote signals or barrier semaphores. Data moves between devices by JAX's collectives and lax.ppermute only.
A program may use at most 128 MiB of HBM per device.

```python
import jax
import jax.numpy as jnp
from jax import lax

PROBES = 256
PART_DEV = 448
BIN_DEV = 2
GROUPS = 16
PIX = 25600
PARTICLES = 28672
BINS = 128
N_DOM = 64


def draw_panels(key, part):

    def one_bin(index):
        bin_key = jax.random.fold_in(key, index)
        key_common, key_single = jax.random.split(bin_key)
        common = jax.random.normal(key_common, (PIX, 1), jnp.float32)
        single = jax.random.normal(key_single, (PIX, PROBES + 2), jnp.float32)
        shared_weight = 0.6
        blended = shared_weight * common + single[:, 0:PROBES] + 0.8 * single[:, 1:PROBES + 1] + 0.5 * single[:, 2:PROBES + 2]
        spread = (1.89 + shared_weight * shared_weight) ** 0.5
        return blended * (1.0 / (spread * PIX ** 0.5))
    return lax.map(one_bin, jnp.arange(BINS, dtype=jnp.int32)).astype(jnp.bfloat16)


def plant(result, rng, smallest, top_value):
    longest = result.shape.index(max(result.shape))
    spots = []
    for shift in (0, 1):
        where = [jax.random.randint(jax.random.fold_in(rng, axis), (), 0, length) for axis, length in enumerate(result.shape)]
        where[longest] = (where[longest] + shift) % result.shape[longest]
        spots.append(tuple(where))
    return result.at[spots[0]].set(smallest).at[spots[1]].set(top_value)


def steps_of(rng, dims, cuts, least, top_value):
    def one(dim, shards_of):
        draws = jax.random.uniform(jax.random.fold_in(jax.random.fold_in(rng, 6), dim), (shards_of,), jnp.float32, least / len(cuts), top_value / len(cuts))
        return jnp.repeat(jnp.exp(draws), dims[dim] // shards_of).reshape((-1,) + (1,) * (len(dims) - dim - 1))

    gain = one(*cuts[0])
    for cut in cuts[1:]:
        gain = gain * one(*cut)
    return gain


def centred(stream_key, shape, scale, bound, cuts=(), kind=jnp.bfloat16):
    level = steps_of(stream_key, shape, cuts, -0.22, 0.18) if cuts else 1.0
    drawn = jax.random.normal(stream_key, shape, jnp.float32) * scale * level
    return jnp.minimum(jnp.maximum(drawn, -bound), bound).astype(kind)


def setup_inputs(seed: int = 0) -> dict:
    splits = jax.random.split(jax.random.key(seed), 7)
    return {
        "images": centred(splits[0], (PARTICLES, PIX), 1.0, 6.0, ((0, 64), (1, 4))),
        "panels": draw_panels(jax.random.fold_in(splits[6], 71), 0),
        "mean_panels": centred(splits[2], (BINS, PIX), 1.0, 6.0, ((0, 64), (1, 4)), jnp.float32),
        "ctf_table": jnp.clip(jax.random.uniform(splits[3], (GROUPS, PIX), jnp.float32, -1.0, 1.0) * steps_of(splits[3], (GROUPS, PIX), ((1, 4),), -0.4, 0.0), -1.0, 1.0),
        "pose_bin": plant(jax.random.randint(splits[4], (PARTICLES,), 0, BIN_DEV), jax.random.fold_in(splits[4], 1), 0, BIN_DEV - 1).astype(jnp.int32),
        "ctf_group": plant(jax.random.randint(splits[5], (PARTICLES,), 0, GROUPS), jax.random.fold_in(splits[5], 1), 0, GROUPS - 1).astype(jnp.int32),
    }


def high_dot(left, right):
    return jnp.dot(left, right, precision=lax.Precision.HIGHEST, preferred_element_type=jnp.float32)

def cholesky_small(matrix):
    order = matrix.shape[0]
    places = jnp.arange(order, dtype=jnp.int32)

    def column_step(index, carry):
        work, lower = carry
        index = jnp.asarray(index).astype(jnp.int32)
        column = lax.dynamic_slice_in_dim(work, index, 1, 1)[:, 0]
        pivot = jnp.sqrt(lax.dynamic_slice_in_dim(column, index, 1, 0)[0])
        below = jnp.where(places > index, column / pivot, jnp.zeros_like(column))
        filled = below + jnp.where(places == index, pivot, jnp.zeros_like(column))
        lower = lower + filled[:, None] * (places == index).astype(matrix.dtype)[None, :]
        work = work - below[:, None] * below[None, :]
        return (work, lower)
    return lax.fori_loop(0, order, column_step, (matrix, jnp.zeros_like(matrix)))[1]

def inverse_small(lower):
    order = lower.shape[0]
    places = jnp.arange(order, dtype=jnp.int32)

    def row_step(index, inverse):
        index = jnp.asarray(index).astype(jnp.int32)
        row_lower = lax.dynamic_slice_in_dim(lower, index, 1, 0)[0]
        pivot = lax.dynamic_slice_in_dim(row_lower, index, 1, 0)[0]
        unit = (places == index).astype(lower.dtype)
        solved = (unit - high_dot(row_lower, inverse)) / pivot
        return inverse + unit[:, None] * solved[None, :]
    return lax.fori_loop(0, order, row_step, jnp.zeros_like(lower))

def assemble(top_left, bottom_left, bottom_right):
    half = top_left.shape[0]
    rest = bottom_right.shape[0]
    upper_part = jnp.concatenate([top_left, jnp.zeros((half, rest), top_left.dtype)], axis=1)
    lower_part = jnp.concatenate([bottom_left, bottom_right], axis=1)
    return jnp.concatenate([upper_part, lower_part], axis=0)

def cholesky_pair(matrix):
    order = matrix.shape[0]
    if order <= 16:
        lower = cholesky_small(matrix)
        return (lower, inverse_small(lower))
    half = order // 2
    lower_a, inverse_a = cholesky_pair(matrix[:half, :half])
    below = high_dot(matrix[half:, :half], inverse_a.T)
    schur = matrix[half:, half:] - high_dot(below, below.T)
    lower_b, inverse_b = cholesky_pair(schur)
    inverse_mid = -high_dot(inverse_b, high_dot(below, inverse_a))
    return (assemble(lower_a, below, lower_b), assemble(inverse_a, inverse_mid, inverse_b))

def lower_inverse(lower):
    order = lower.shape[0]
    if order <= 16:
        return inverse_small(lower)
    half = order // 2
    inverse_a = lower_inverse(lower[:half, :half])
    inverse_b = lower_inverse(lower[half:, half:])
    inverse_mid = -high_dot(inverse_b, high_dot(lower[half:, :half], inverse_a))
    return assemble(inverse_a, inverse_mid, inverse_b)

def weighted_block(images_block, pose_block, group_block, panel_block, mean_block, ctf_table):
    ctf_rows = jnp.take(ctf_table, group_block.astype(jnp.int32), axis=0)
    mean_rows = jnp.take(mean_block, pose_block.astype(jnp.int32), axis=0)
    weighted = (ctf_rows * (images_block.astype(jnp.float32) - ctf_rows * mean_rows)).astype(jnp.bfloat16)
    coeffs = jnp.zeros((images_block.shape[0], panel_block.shape[2]), jnp.float32)
    for which in range(BIN_DEV):
        chosen = jnp.where((pose_block == which)[:, None], weighted, jnp.zeros_like(weighted))
        coeffs = coeffs + jnp.dot(chosen, panel_block[which], preferred_element_type=jnp.float32)
    return coeffs

def reference(images, panels, mean_panels, ctf_table, pose_bin, ctf_group):
    images_r = images.reshape(N_DOM, PART_DEV, PIX)
    pose_r = pose_bin.reshape(N_DOM, PART_DEV)
    group_r = ctf_group.reshape(N_DOM, PART_DEV)
    panels_r = panels.reshape(N_DOM, BIN_DEV, PIX, PROBES)
    means_r = mean_panels.reshape(N_DOM, BIN_DEV, PIX)

    def one_block(pieces):
        return weighted_block(pieces[0], pieces[1], pieces[2], pieces[3], pieces[4], ctf_table)
    coeffs = lax.map(one_block, (images_r, pose_r, group_r, panels_r, means_r)).reshape(PARTICLES, PROBES)
    gram = high_dot(coeffs.T, coeffs) / PARTICLES
    lower, inverse = cholesky_pair(gram)
    scores = jnp.dot(coeffs, inverse.T, precision=lax.Precision.HIGHEST)
    return (scores, lower.T)
```

```python
import functools

import jax
import jax.numpy as jnp
from jax import lax
from jax.experimental import pallas as pl
from jax.experimental.pallas import tpu as pltpu
from jax.sharding import Mesh, PartitionSpec as P

F32 = jnp.float32
BF16 = jnp.bfloat16
HIGHEST = lax.Precision.HIGHEST

PART = 448
PIECE = 112
PIX = 6400
CHUNK = 640
GROUPS = 16
PROBES = 256


def three_terms(value):
    high = value.astype(BF16)
    rest = value - high.astype(F32)
    middle = rest.astype(BF16)
    low = (rest - middle.astype(F32)).astype(BF16)
    return high, middle, low


def project_kernel(
    place_ref, images_ref, panels_ref, mean_ref, ctf_ref, pose_ref, group_ref,
    own_ref, next_ref, across_ref, before_ref, total, picks, whole,
):
    step = pl.program_id(0)

    @pl.when(step == 0)
    def _():
        rows = lax.broadcasted_iota(jnp.int32, (128, PART), 0)
        group = jnp.broadcast_to(group_ref[...], (128, PART))
        pose = jnp.broadcast_to(pose_ref[...], (128, PART))
        wanted = jnp.where(rows < 3 * GROUPS, lax.rem(rows, GROUPS), 1)
        found = jnp.where(rows < 3 * GROUPS, group, pose)
        picks[...] = jnp.where(wanted == found, 1.0, 0.0).astype(F32).T
        total[...] = jnp.zeros_like(total)

    second = picks[:, 3 * GROUPS : 3 * GROUPS + 1] > 0.5
    stack = jnp.concatenate(three_terms(ctf_ref[...]), axis=0)
    ctf = jnp.dot(picks[:, : 3 * GROUPS].astype(BF16), stack, preferred_element_type=F32)
    mean = jnp.where(second, mean_ref[1:2, :], mean_ref[0:1, :])
    weighted = (ctf * (images_ref[...].astype(F32) - ctf * mean)).astype(BF16)
    for which in range(2):
        total[which] += jnp.dot(weighted, panels_ref[which], preferred_element_type=F32)

    @pl.when(step == pl.num_programs(0) - 1)
    def _():
        whole[...] = jnp.where(second, total[1], total[0])
        place = place_ref[0]
        for shift, out in enumerate((own_ref, next_ref, across_ref, before_ref)):
            first = pl.multiple_of(lax.rem(place + shift, 4) * PIECE, 16)
            out[...] = whole[pl.ds(first, PIECE), :]


def project(place, images, panels, mean_panels, ctf_table, pose_bin, ctf_group):
    piece = jax.ShapeDtypeStruct((PIECE, PROBES), F32)
    whole_piece = pl.BlockSpec((PIECE, PROBES), lambda k: (0, 0))
    return pl.pallas_call(
        project_kernel,
        grid=(PIX // CHUNK,),
        out_shape=(piece,) * 4,
        in_specs=[
            pl.BlockSpec(memory_space=pltpu.SMEM),
            pl.BlockSpec((PART, CHUNK), lambda k: (0, k)),
            pl.BlockSpec((2, CHUNK, PROBES), lambda k: (0, k, 0)),
            pl.BlockSpec((2, CHUNK), lambda k: (0, k)),
            pl.BlockSpec((GROUPS, CHUNK), lambda k: (0, k)),
            pl.BlockSpec((1, PART), lambda k: (0, 0)),
            pl.BlockSpec((1, PART), lambda k: (0, 0)),
        ],
        out_specs=(whole_piece,) * 4,
        scratch_shapes=[
            pltpu.VMEM((2, PART, PROBES), F32),
            pltpu.VMEM((PART, 128), F32),
            pltpu.VMEM((PART, PROBES), F32),
        ],
        compiler_params=pltpu.CompilerParams(vmem_limit_bytes=60 * 1024 * 1024),
        name="project",
    )(place, images, panels, mean_panels, ctf_table, pose_bin.reshape(1, PART), ctf_group.reshape(1, PART))


def gram_kernel(own_ref, first_ref, second_ref, third_ref, coeffs_ref, gram_ref, *, particles):
    coeffs = (own_ref[...] + first_ref[...]) + (second_ref[...] + third_ref[...])
    coeffs_ref[...] = coeffs
    gram = lax.dot_general(
        coeffs, coeffs, (((0,), (0,)), ((), ())), precision=HIGHEST, preferred_element_type=F32
    )
    gram_ref[...] = gram / particles


def gram_of(pieces, particles):
    return pl.pallas_call(
        functools.partial(gram_kernel, particles=particles),
        out_shape=(
            jax.ShapeDtypeStruct((PIECE, PROBES), F32),
            jax.ShapeDtypeStruct((PROBES, PROBES), F32),
        ),
        name="gram",
    )(*pieces)


def factor_kernel(place_ref, gram_ref, c0_ref, c1_ref, c2_ref, c3_ref, scores_ref, factor_ref, work, inv):
    lane = lax.broadcasted_iota(jnp.int32, (256, 256), 1)
    row = lax.broadcasted_iota(jnp.int32, (256, 256), 0)
    work[...] = gram_ref[...]
    inv[...] = jnp.where(lane == row, 1.0, 0.0).astype(F32)
    sub = lax.broadcasted_iota(jnp.int32, (8, 128), 0)

    def spread(value):
        return jnp.broadcast_to(value, (8, 128))

    for block in range(8):
        start = 32 * block
        half = block // 4
        if half == 0:
            tiles = ((work, 0), (work, 128), (inv, 0))
        else:
            tiles = ((work, 128), (inv, 0), (inv, 128))
        rows = [
            [ref[start + 8 * g : start + 8 * g + 8, col : col + 128] for ref, col in tiles]
            for g in range(4)
        ]
        for g in range(4):
            at = start - 128 * half + 8 * g
            cols = [
                {h: spread(rows[h][0][:, at + k : at + k + 1]) for h in range(g, 4)} for k in range(8)
            ]
            pivots = jnp.ones((8, 128), F32)
            for k in range(8):
                heads = {j: spread(cols[j][g][k : k + 1, :]) for j in range(k, 8)}
                pivots = jnp.where(sub == k, heads[k], pivots)
                inverse = 1.0 / heads[k]
                ratio = {h: cols[k][h] * inverse for h in range(g, 4)}
                ratio[g] = jnp.where(sub > k, ratio[g], 0.0)
                for j in range(k + 1, 8):
                    for h in range(g, 4):
                        cols[j][h] = cols[j][h] - ratio[h] * heads[j]
                for t in range(3):
                    head = spread(rows[g][t][k : k + 1, :])
                    for h in range(g, 4):
                        rows[h][t] = rows[h][t] - ratio[h] * head
            scale = lax.rsqrt(pivots)
            rows[g] = [value * scale for value in rows[g]]
        done = [jnp.concatenate([rows[g][t] for g in range(4)], axis=0) for t in range(3)]
        for (ref, col), value in zip(tiles, done):
            ref[start : start + 32, col : col + 128] = value
        if block == 7:
            break
        terms = [three_terms(value) for value in done]

        def left(t):
            high, middle, low = terms[t]
            return jnp.concatenate([high, high, middle, high, middle, low], axis=0)

        def right(ts):
            high, middle, low = (jnp.concatenate([terms[t][i] for t in ts], axis=1) for i in range(3))
            return jnp.concatenate([high, middle, high, low, middle, high], axis=0)

        def product(t, ts):
            return lax.dot_general(
                left(t), right(ts), (((0,), (0,)), ((), ())), preferred_element_type=F32
            )

        inside = start - 128 * half + 32
        if inside < 128:
            change = product(0, (0, 1, 2))
            for t, (ref, col) in enumerate(tiles):
                ref[start + 32 : 128 * half + 128, col : col + 128] -= change[inside:, 128 * t : 128 * t + 128]
        if half == 0:
            change = product(1, (1, 2))
            for t, (ref, col) in enumerate(tiles[1:]):
                ref[128:256, col : col + 128] -= change[:, 128 * t : 128 * t + 128]

    factor_ref[...] = jnp.where(row <= lane, work[...], 0.0)
    inverse = inv[...]
    place = place_ref[0]
    for shift, coeffs in enumerate((c0_ref, c1_ref, c2_ref, c3_ref)):
        first = pl.multiple_of(lax.rem(place + shift, 4) * PIECE, 16)
        scores_ref[pl.ds(first, PIECE), :] = lax.dot_general(
            coeffs[...], inverse, (((1,), (1,)), ((), ())), precision=HIGHEST, preferred_element_type=F32
        )


def factor_and_scores(place, gram, pieces):
    vmem = pl.BlockSpec(memory_space=pltpu.VMEM)
    return pl.pallas_call(
        factor_kernel,
        out_shape=(
            jax.ShapeDtypeStruct((PART, PROBES), F32),
            jax.ShapeDtypeStruct((PROBES, PROBES), F32),
        ),
        in_specs=[pl.BlockSpec(memory_space=pltpu.SMEM)] + [vmem] * 5,
        out_specs=(vmem, vmem),
        scratch_shapes=[pltpu.VMEM((PROBES, PROBES), F32), pltpu.VMEM((PROBES, PROBES), F32)],
        compiler_params=pltpu.CompilerParams(vmem_limit_bytes=32 * 1024 * 1024),
        name="factor",
    )(place, gram, *pieces)


def shifted(value, shift):
    return lax.ppermute(value, "x", [(i, (i + shift) % 4) for i in range(4)])


def sum_everywhere(gram):
    cut = gram.reshape(16, 16, PROBES)
    part = lax.all_to_all(cut, ("y", "x"), 0, 0, tiled=True).sum(0)
    part = part + lax.ppermute(part, "core", [(0, 1), (1, 0)])
    copies = jnp.broadcast_to(part[None], (8, 16, PROBES))
    part = lax.all_to_all(copies, "z", 0, 0, tiled=True).sum(0)
    copies = jnp.broadcast_to(part[None], (16, 16, PROBES))
    return lax.all_to_all(copies, ("y", "x"), 0, 0, tiled=True).reshape(PROBES, PROBES)


def body(images, panels, mean_panels, ctf_table, pose_bin, ctf_group):
    place = lax.axis_index("x").astype(jnp.int32).reshape(1)
    particles = PART * 64
    own, following, across, before = project(
        place, images, panels, mean_panels, ctf_table, pose_bin, ctf_group
    )
    across = shifted(across, 2)
    following = shifted(following, 1)
    before = shifted(before, 3)
    coeffs, gram = gram_of((own, following, across, before), particles)
    pieces = (coeffs, shifted(coeffs, 3), shifted(coeffs, 2), shifted(coeffs, 1))
    gram = sum_everywhere(gram)
    return factor_and_scores(place, gram, pieces)


def solution(mesh):
    fine = Mesh(mesh.devices.reshape(8, 4, 2, 4), ("z", "y", "core", "x"))
    dom = ("z", "y", "core")
    placed = (
        P(dom, "x"),
        P(dom, "x", None),
        P(dom, "x"),
        P(None, "x"),
        P(dom),
        P(dom),
    )
    return jax.shard_map(
        body, mesh=fine, in_specs=placed, out_specs=(P(dom, None), P()), check_vma=False
    )
```

```python
import functools

import jax
import jax.numpy as jnp
from jax import lax
from jax.experimental import pallas as pl
from jax.experimental.pallas import tpu as pltpu
from jax.sharding import Mesh, PartitionSpec as P

F32 = jnp.float32
BF16 = jnp.bfloat16
HIGHEST = lax.Precision.HIGHEST

PART = 448
PIECE = 112
PIX = 6400
CUTS = (0, 2048, 4352, 6400)
STEP = 1280
GROUPS = 16
PROBES = 256
HALF = 192


def three_terms(value):
    high = value.astype(BF16)
    rest = value - high.astype(F32)
    middle = rest.astype(BF16)
    low = (rest - middle.astype(F32)).astype(BF16)
    return high, middle, low


def project_kernel(
    place_ref, pose_ref, group_ref, images_ref, panels_ref, mean_ref, ctf_ref,
    own_ref, next_ref, across_ref, before_ref,
    images, panels, mean, ctf, weighted, total, picks, whole, sems,
):
    chunks = [slice(first, last) for first, last in zip(CUTS[:-1], CUTS[1:])]
    copies = []
    for i, cut in enumerate(chunks):
        pairs = (
            (ctf_ref.at[:, cut], ctf.at[:, cut]),
            (mean_ref.at[:, cut], mean.at[:, cut]),
            (images_ref.at[:, cut], images.at[:, cut]),
            (panels_ref.at[0, cut, :], panels.at[0, cut, :]),
            (panels_ref.at[1, cut, :], panels.at[1, cut, :]),
        )
        copies.append([pltpu.make_async_copy(*pair, sems.at[i, j]) for j, pair in enumerate(pairs)])
    for copy in copies[0]:
        copy.start()

    rows = lax.broadcasted_iota(jnp.int32, (128, PART), 0)
    group = jnp.broadcast_to(group_ref[...], (128, PART))
    pose = jnp.broadcast_to(pose_ref[...], (128, PART))
    wanted = jnp.where(rows < 3 * GROUPS, lax.rem(rows, GROUPS), 1)
    found = jnp.where(rows < 3 * GROUPS, group, pose)
    picks[...] = jnp.where(wanted == found, 1.0, 0.0).astype(F32).T
    second = picks[:, 3 * GROUPS : 3 * GROUPS + 1] > 0.5
    chosen = picks[:, : 3 * GROUPS].astype(BF16)

    def weigh(cut):
        stack = jnp.concatenate(three_terms(ctf[:, cut]), axis=0)
        factor = jnp.dot(chosen, stack, preferred_element_type=F32)
        middle = jnp.where(second, mean[1:2, cut], mean[0:1, cut])
        weighted[:, cut] = (factor * (images[:, cut].astype(F32) - factor * middle)).astype(BF16)

    def add(cut):
        for which in range(2):
            part = jnp.dot(weighted[:, cut], panels[which, cut, :], preferred_element_type=F32)
            total[which] = part if cut.start == 0 else total[which] + part

    for i, chunk in enumerate(chunks):
        for copy in copies[i]:
            copy.wait()
        if i + 1 < len(chunks):
            for copy in copies[i + 1]:
                copy.start()
        cuts = [slice(at, min(at + STEP, chunk.stop)) for at in range(chunk.start, chunk.stop, STEP)]
        weigh(cuts[0])
        for j, cut in enumerate(cuts):
            if j + 1 < len(cuts):
                weigh(cuts[j + 1])
            add(cut)
    whole[...] = jnp.where(second, total[1], total[0])
    place = place_ref[0]
    for shift, out in enumerate((own_ref, next_ref, across_ref, before_ref)):
        first = pl.multiple_of(lax.rem(place + shift, 4) * PIECE, 16)
        out[...] = whole[pl.ds(first, PIECE), :]


def project(place, images, panels, mean_panels, ctf_table, pose_bin, ctf_group):
    piece = jax.ShapeDtypeStruct((PIECE, PROBES), F32)
    vmem = pl.BlockSpec(memory_space=pltpu.VMEM)
    anywhere = pl.BlockSpec(memory_space=pl.ANY)
    return pl.pallas_call(
        project_kernel,
        out_shape=(piece,) * 4,
        in_specs=[pl.BlockSpec(memory_space=pltpu.SMEM), vmem, vmem] + [anywhere] * 4,
        out_specs=(vmem,) * 4,
        scratch_shapes=[
            pltpu.VMEM((PART, PIX), BF16),
            pltpu.VMEM((2, PIX, PROBES), BF16),
            pltpu.VMEM((2, PIX), F32),
            pltpu.VMEM((GROUPS, PIX), F32),
            pltpu.VMEM((PART, PIX), BF16),
            pltpu.VMEM((2, PART, PROBES), F32),
            pltpu.VMEM((PART, 128), F32),
            pltpu.VMEM((PART, PROBES), F32),
            pltpu.SemaphoreType.DMA((len(CUTS) - 1, 5)),
        ],
        compiler_params=pltpu.CompilerParams(vmem_limit_bytes=60 * 1024 * 1024),
        name="project",
    )(place, pose_bin.reshape(1, PART), ctf_group.reshape(1, PART), images, panels, mean_panels, ctf_table)


def gram_kernel(core_ref, own_ref, first_ref, second_ref, third_ref, coeffs_ref, mine_ref, other_ref, packed, *, particles):
    coeffs = (own_ref[...] + first_ref[...]) + (second_ref[...] + third_ref[...])
    coeffs_ref[...] = coeffs

    def block(left, right):
        gram = lax.dot_general(
            left, right, (((0,), (0,)), ((), ())), precision=HIGHEST, preferred_element_type=F32
        )
        return gram / particles

    top = block(coeffs[:, :128], coeffs)
    packed[:128, :] = top[:, :128]
    packed[128:256, :] = top[:, 128:]
    packed[256:, :] = block(coeffs[:, 128:], coeffs[:, 128:])
    core = core_ref[0]
    mine_ref[...] = packed[pl.ds(pl.multiple_of(core * HALF, 8), HALF), :]
    other_ref[...] = packed[pl.ds(pl.multiple_of((1 - core) * HALF, 8), HALF), :]


def gram_of(core, pieces, particles):
    vmem = pl.BlockSpec(memory_space=pltpu.VMEM)
    return pl.pallas_call(
        functools.partial(gram_kernel, particles=particles),
        out_shape=(
            jax.ShapeDtypeStruct((PIECE, PROBES), F32),
            jax.ShapeDtypeStruct((HALF, 128), F32),
            jax.ShapeDtypeStruct((HALF, 128), F32),
        ),
        in_specs=[pl.BlockSpec(memory_space=pltpu.SMEM)] + [vmem] * 4,
        out_specs=(vmem,) * 3,
        scratch_shapes=[pltpu.VMEM((2 * HALF, 128), F32)],
        compiler_params=pltpu.CompilerParams(vmem_limit_bytes=12 * 1024 * 1024),
        name="gram",
    )(core, *pieces)


def factor_kernel(
    place_ref, core_ref, mine_ref, other_ref, c0_ref, c1_ref, c2_ref, c3_ref, scores_ref, factor_ref, work, inv
):
    lane = lax.broadcasted_iota(jnp.int32, (256, 256), 1)
    row = lax.broadcasted_iota(jnp.int32, (256, 256), 0)
    core = core_ref[0]
    work[pl.ds(pl.multiple_of(core * HALF, 8), HALF), :] = mine_ref[...]
    work[pl.ds(pl.multiple_of((1 - core) * HALF, 8), HALF), :] = other_ref[...]
    inv[...] = jnp.where(lane == row, 1.0, 0.0).astype(F32)
    sub = lax.broadcasted_iota(jnp.int32, (8, 128), 0)

    def spread(value):
        return jnp.broadcast_to(value, (8, 128))

    for block in range(8):
        start = 32 * block
        half = block // 4
        if half == 0:
            tiles = ((work, 0, 0), (work, 128, 0), (inv, 0, 0))
        else:
            tiles = ((work, 128, 0), (inv, 0, 0), (inv, 0, 128))
        rows = [
            [ref[start + low + 8 * g : start + low + 8 * g + 8, col : col + 128] for ref, low, col in tiles]
            for g in range(4)
        ]
        for g in range(4):
            at = start - 128 * half + 8 * g
            cols = [
                {h: spread(rows[h][0][:, at + k : at + k + 1]) for h in range(g, 4)} for k in range(8)
            ]
            pivots = jnp.ones((8, 128), F32)
            for k in range(8):
                heads = {j: spread(cols[j][g][k : k + 1, :]) for j in range(k, 8)}
                pivots = jnp.where(sub == k, heads[k], pivots)
                inverse = 1.0 / heads[k]
                ratio = {h: cols[k][h] * inverse for h in range(g, 4)}
                ratio[g] = jnp.where(sub > k, ratio[g], 0.0)
                for j in range(k + 1, 8):
                    for h in range(g, 4):
                        cols[j][h] = cols[j][h] - ratio[h] * heads[j]
                for t in range(3):
                    head = spread(rows[g][t][k : k + 1, :])
                    for h in range(g, 4):
                        rows[h][t] = rows[h][t] - ratio[h] * head
            scale = lax.rsqrt(pivots)
            rows[g] = [value * scale for value in rows[g]]
        done = [jnp.concatenate([rows[g][t] for g in range(4)], axis=0) for t in range(3)]
        for (ref, low, col), value in zip(tiles, done):
            ref[start + low : start + low + 32, col : col + 128] = value
        if block == 7:
            break
        terms = [three_terms(value) for value in done]

        def left(t):
            high, middle, low = terms[t]
            return jnp.concatenate([high, high, middle, high, middle, low], axis=0)

        def right(ts):
            high, middle, low = (jnp.concatenate([terms[t][i] for t in ts], axis=1) for i in range(3))
            return jnp.concatenate([high, middle, high, low, middle, high], axis=0)

        def product(t, ts):
            return lax.dot_general(
                left(t), right(ts), (((0,), (0,)), ((), ())), preferred_element_type=F32
            )

        inside = start - 128 * half + 32
        if inside < 128:
            change = product(0, (0, 1, 2))
            for t, (ref, low, col) in enumerate(tiles):
                last = 128 * half + 128 + low
                ref[start + 32 + low : last, col : col + 128] -= change[inside:, 128 * t : 128 * t + 128]
        if half == 0:
            change = product(1, (1, 2))
            for t, (ref, low, col) in enumerate(tiles[1:]):
                ref[128 + low : 256 + low, col : col + 128] -= change[:, 128 * t : 128 * t + 128]

    upper = row[:128, :128] <= lane[:128, :128]
    factor_ref[:128, :128] = jnp.where(upper, work[:128, :], 0.0)
    factor_ref[:128, 128:] = work[128:256, :]
    factor_ref[128:, :128] = jnp.zeros((128, 128), F32)
    factor_ref[128:, 128:] = jnp.where(upper, work[256:, :], 0.0)
    inverse = inv[...]
    place = place_ref[0]
    for shift, coeffs in enumerate((c0_ref, c1_ref, c2_ref, c3_ref)):
        first = pl.multiple_of(lax.rem(place + shift, 4) * PIECE, 16)
        scores_ref[pl.ds(first, PIECE), :] = lax.dot_general(
            coeffs[...], inverse, (((1,), (1,)), ((), ())), precision=HIGHEST, preferred_element_type=F32
        )


def factor_and_scores(place, core, halves, pieces):
    vmem = pl.BlockSpec(memory_space=pltpu.VMEM)
    return pl.pallas_call(
        factor_kernel,
        out_shape=(
            jax.ShapeDtypeStruct((PART, PROBES), F32),
            jax.ShapeDtypeStruct((PROBES, PROBES), F32),
        ),
        in_specs=[pl.BlockSpec(memory_space=pltpu.SMEM)] * 2 + [vmem] * 6,
        out_specs=(vmem, vmem),
        scratch_shapes=[pltpu.VMEM((2 * HALF, 128), F32), pltpu.VMEM((PROBES, PROBES), F32)],
        compiler_params=pltpu.CompilerParams(vmem_limit_bytes=12 * 1024 * 1024),
        name="factor",
    )(place, core, *halves, *pieces)


def shifted(value, shift):
    return lax.ppermute(value, "x", [(i, (i + shift) % 4) for i in range(4)])


def partner_of(step, z, y, core, x):
    if step < 4:
        flip = (1, 3)[step % 2]
        return (z, y, core, x ^ flip) if (step < 2) == (core == 0) else (z, y ^ flip, core, x)
    return (z ^ (1, 2, 6)[step - 4], y, core, x)


def exchanged(value, step):
    moves = []
    for z in range(8):
        for y in range(4):
            for core in range(2):
                for x in range(4):
                    to_z, to_y, to_core, to_x = partner_of(step, z, y, core, x)
                    source = ((z * 4 + y) * 2 + core) * 4 + x
                    moves.append((source, ((to_z * 4 + to_y) * 2 + to_core) * 4 + to_x))
    return lax.ppermute(value, ("z", "y", "core", "x"), moves)


def other_core(value):
    return lax.ppermute(value, "core", [(0, 1), (1, 0)])


def sum_everywhere(mine, other, coeffs):
    part = mine + other_core(other)
    for step in range(4):
        part = part + exchanged(part, step)
    pieces = []
    for step in range(4, 7):
        piece = shifted(coeffs, (2, 3, 1)[step - 4])
        part, piece = lax.optimization_barrier((part + exchanged(part, step), piece))
        pieces.append(piece)
    across, following, before = pieces
    return (part, other_core(part)), (following, across, before)


def body(images, panels, mean_panels, ctf_table, pose_bin, ctf_group):
    place = lax.axis_index("x").astype(jnp.int32).reshape(1)
    core = lax.axis_index("core").astype(jnp.int32).reshape(1)
    particles = PART * 64
    own, following, across, before = project(
        place, images, panels, mean_panels, ctf_table, pose_bin, ctf_group
    )
    across = shifted(across, 2)
    following = shifted(following, 1)
    before = shifted(before, 3)
    coeffs, mine, other = gram_of(core, (own, following, across, before), particles)
    halves, pieces = sum_everywhere(mine, other, coeffs)
    return factor_and_scores(place, core, halves, (coeffs, *pieces))


def solution(mesh):
    fine = Mesh(mesh.devices.reshape(8, 4, 2, 4), ("z", "y", "core", "x"))
    dom = ("z", "y", "core")
    placed = (
        P(dom, "x"),
        P(dom, "x", None),
        P(dom, "x"),
        P(None, "x"),
        P(dom),
        P(dom),
    )
    return jax.shard_map(
        body, mesh=fine, in_specs=placed, out_specs=(P(dom, None), P()), check_vma=False
    )
```

```python
import functools

import jax
import jax.numpy as jnp
from jax import lax
from jax.experimental import pallas as pl
from jax.experimental.pallas import tpu as pltpu
from jax.sharding import Mesh, PartitionSpec as P

F32 = jnp.float32
BF16 = jnp.bfloat16
HIGHEST = lax.Precision.HIGHEST

PART = 448
PIECE = 112
PIX = 6400
CUTS = (0, 2048, 4352, 6400)
STEP = 1280
GROUPS = 16
PROBES = 256
HALF = 192


def three_terms(value):
    high = value.astype(BF16)
    rest = value - high.astype(F32)
    middle = rest.astype(BF16)
    low = (rest - middle.astype(F32)).astype(BF16)
    return high, middle, low


def project_kernel(
    pose_ref, group_ref, images_ref, panels_ref, mean_ref, ctf_ref,
    own_ref, next_ref, across_ref, before_ref,
    pose_in, group_in, images, panels, mean, ctf, weighted, total, picks, whole, sems, index_sems,
):
    chunks = [slice(first, last) for first, last in zip(CUTS[:-1], CUTS[1:])]
    copies = []
    for i, cut in enumerate(chunks):
        pairs = (
            (ctf_ref.at[:, cut], ctf.at[:, cut]),
            (mean_ref.at[:, cut], mean.at[:, cut]),
            (images_ref.at[:, cut], images.at[:, cut]),
            (panels_ref.at[0, cut, :], panels.at[0, cut, :]),
            (panels_ref.at[1, cut, :], panels.at[1, cut, :]),
        )
        copies.append([pltpu.make_async_copy(*pair, sems.at[i, j]) for j, pair in enumerate(pairs)])
    indices = (
        pltpu.make_async_copy(pose_ref, pose_in, index_sems.at[0]),
        pltpu.make_async_copy(group_ref, group_in, index_sems.at[1]),
    )
    for copy in (*indices, *copies[0]):
        copy.start()
    for copy in indices:
        copy.wait()

    rows = lax.broadcasted_iota(jnp.int32, (128, PART), 0)
    group = jnp.broadcast_to(group_in[...], (128, PART))
    pose = jnp.broadcast_to(pose_in[...], (128, PART))
    wanted = jnp.where(rows < 3 * GROUPS, lax.rem(rows, GROUPS), 1)
    found = jnp.where(rows < 3 * GROUPS, group, pose)
    picks[...] = jnp.where(wanted == found, 1.0, 0.0).astype(F32).T
    second = picks[:, 3 * GROUPS : 3 * GROUPS + 1] > 0.5
    chosen = picks[:, : 3 * GROUPS].astype(BF16)

    def weigh(cut):
        stack = jnp.concatenate(three_terms(ctf[:, cut]), axis=0)
        factor = jnp.dot(chosen, stack, preferred_element_type=F32)
        middle = jnp.where(second, mean[1:2, cut], mean[0:1, cut])
        weighted[:, cut] = (factor * (images[:, cut].astype(F32) - factor * middle)).astype(BF16)

    def add(cut):
        for which in range(2):
            part = jnp.dot(weighted[:, cut], panels[which, cut, :], preferred_element_type=F32)
            total[which] = part if cut.start == 0 else total[which] + part

    for i, chunk in enumerate(chunks):
        for copy in copies[i][:3]:
            copy.wait()
        if i + 1 < len(chunks):
            for copy in copies[i + 1]:
                copy.start()
        cuts = [slice(at, min(at + STEP, chunk.stop)) for at in range(chunk.start, chunk.stop, STEP)]
        weigh(cuts[0])
        for copy in copies[i][3:]:
            copy.wait()
        for j, cut in enumerate(cuts):
            if j + 1 < len(cuts):
                weigh(cuts[j + 1])
            add(cut)
    whole[...] = jnp.where(second, total[1], total[0])
    place = lax.axis_index("x")
    for shift, out in enumerate((own_ref, next_ref, across_ref, before_ref)):
        first = pl.multiple_of(lax.rem(place + shift, 4) * PIECE, 16)
        out[...] = whole[pl.ds(first, PIECE), :]


def project(images, panels, mean_panels, ctf_table, pose_bin, ctf_group):
    piece = jax.ShapeDtypeStruct((PIECE, PROBES), F32)
    vmem = pl.BlockSpec(memory_space=pltpu.VMEM)
    anywhere = pl.BlockSpec(memory_space=pl.ANY)
    return pl.pallas_call(
        project_kernel,
        out_shape=(piece,) * 4,
        in_specs=[anywhere] * 6,
        out_specs=(vmem,) * 4,
        scratch_shapes=[
            pltpu.VMEM((1, PART), jnp.int32),
            pltpu.VMEM((1, PART), jnp.int32),
            pltpu.VMEM((PART, PIX), BF16),
            pltpu.VMEM((2, PIX, PROBES), BF16),
            pltpu.VMEM((2, PIX), F32),
            pltpu.VMEM((GROUPS, PIX), F32),
            pltpu.VMEM((PART, PIX), BF16),
            pltpu.VMEM((2, PART, PROBES), F32),
            pltpu.VMEM((PART, 128), F32),
            pltpu.VMEM((PART, PROBES), F32),
            pltpu.SemaphoreType.DMA((len(CUTS) - 1, 5)),
            pltpu.SemaphoreType.DMA((2,)),
        ],
        compiler_params=pltpu.CompilerParams(vmem_limit_bytes=60 * 1024 * 1024),
        name="project",
    )(pose_bin.reshape(1, PART), ctf_group.reshape(1, PART), images, panels, mean_panels, ctf_table)


def keep_kernel(piece_ref, kept_ref):
    kept_ref[...] = piece_ref[...]


def kept(piece):
    vmem = pl.BlockSpec(memory_space=pltpu.VMEM)
    return pl.pallas_call(
        keep_kernel,
        out_shape=jax.ShapeDtypeStruct(piece.shape, piece.dtype),
        in_specs=[vmem],
        out_specs=vmem,
        compiler_params=pltpu.CompilerParams(vmem_limit_bytes=2 * 1024 * 1024),
        name="keep",
    )(piece)


def gram_kernel(core_ref, own_ref, first_ref, second_ref, third_ref, coeffs_ref, mine_ref, other_ref, packed, *, particles):
    coeffs = (own_ref[...] + first_ref[...]) + (second_ref[...] + third_ref[...])
    coeffs_ref[...] = coeffs

    def block(left, right):
        gram = lax.dot_general(
            left, right, (((0,), (0,)), ((), ())), precision=HIGHEST, preferred_element_type=F32
        )
        return gram / particles

    top = block(coeffs[:, :128], coeffs)
    packed[:128, :] = top[:, :128]
    packed[128:256, :] = top[:, 128:]
    packed[256:, :] = block(coeffs[:, 128:], coeffs[:, 128:])
    core = core_ref[0]
    mine_ref[...] = packed[pl.ds(pl.multiple_of(core * HALF, 8), HALF), :]
    other_ref[...] = packed[pl.ds(pl.multiple_of((1 - core) * HALF, 8), HALF), :]


def gram_of(core, pieces, particles):
    vmem = pl.BlockSpec(memory_space=pltpu.VMEM)
    return pl.pallas_call(
        functools.partial(gram_kernel, particles=particles),
        out_shape=(
            jax.ShapeDtypeStruct((PIECE, PROBES), F32),
            jax.ShapeDtypeStruct((HALF, 128), F32),
            jax.ShapeDtypeStruct((HALF, 128), F32),
        ),
        in_specs=[pl.BlockSpec(memory_space=pltpu.SMEM)] + [vmem] * 4,
        out_specs=(vmem,) * 3,
        scratch_shapes=[pltpu.VMEM((2 * HALF, 128), F32)],
        compiler_params=pltpu.CompilerParams(vmem_limit_bytes=12 * 1024 * 1024),
        name="gram",
    )(core, *pieces)


def factor_kernel(
    place_ref, core_ref, mine_ref, other_ref, c0_ref, c1_ref, c2_ref, c3_ref, scores_ref, factor_ref, work, inv
):
    lane = lax.broadcasted_iota(jnp.int32, (256, 256), 1)
    row = lax.broadcasted_iota(jnp.int32, (256, 256), 0)
    core = core_ref[0]
    work[pl.ds(pl.multiple_of(core * HALF, 8), HALF), :] = mine_ref[...]
    work[pl.ds(pl.multiple_of((1 - core) * HALF, 8), HALF), :] = other_ref[...]
    inv[...] = jnp.where(lane == row, 1.0, 0.0).astype(F32)
    sub = lax.broadcasted_iota(jnp.int32, (8, 128), 0)

    def spread(value):
        return jnp.broadcast_to(value, (8, 128))

    for block in range(8):
        start = 32 * block
        half = block // 4
        if half == 0:
            tiles = ((work, 0, 0), (work, 128, 0), (inv, 0, 0))
        else:
            tiles = ((work, 128, 0), (inv, 0, 0), (inv, 0, 128))
        rows = [
            [ref[start + low + 8 * g : start + low + 8 * g + 8, col : col + 128] for ref, low, col in tiles]
            for g in range(4)
        ]
        for g in range(4):
            at = start - 128 * half + 8 * g
            cols = [
                {h: spread(rows[h][0][:, at + k : at + k + 1]) for h in range(g, 4)} for k in range(8)
            ]
            pivots = jnp.ones((8, 128), F32)
            for k in range(8):
                heads = {j: spread(cols[j][g][k : k + 1, :]) for j in range(k, 8)}
                pivots = jnp.where(sub == k, heads[k], pivots)
                inverse = 1.0 / heads[k]
                ratio = {h: cols[k][h] * inverse for h in range(g, 4)}
                ratio[g] = jnp.where(sub > k, ratio[g], 0.0)
                for j in range(k + 1, 8):
                    for h in range(g, 4):
                        cols[j][h] = cols[j][h] - ratio[h] * heads[j]
                for t in range(3):
                    head = spread(rows[g][t][k : k + 1, :])
                    for h in range(g, 4):
                        rows[h][t] = rows[h][t] - ratio[h] * head
            scale = lax.rsqrt(pivots)
            rows[g] = [value * scale for value in rows[g]]
        done = [jnp.concatenate([rows[g][t] for g in range(4)], axis=0) for t in range(3)]
        for (ref, low, col), value in zip(tiles, done):
            ref[start + low : start + low + 32, col : col + 128] = value
        if block == 7:
            break
        terms = [three_terms(value) for value in done]

        def left(t):
            high, middle, low = terms[t]
            return jnp.concatenate([high, high, middle, high, middle, low], axis=0)

        def right(ts):
            high, middle, low = (jnp.concatenate([terms[t][i] for t in ts], axis=1) for i in range(3))
            return jnp.concatenate([high, middle, high, low, middle, high], axis=0)

        def product(t, ts):
            return lax.dot_general(
                left(t), right(ts), (((0,), (0,)), ((), ())), preferred_element_type=F32
            )

        inside = start - 128 * half + 32
        if inside < 128:
            change = product(0, (0, 1, 2))
            for t, (ref, low, col) in enumerate(tiles):
                last = 128 * half + 128 + low
                ref[start + 32 + low : last, col : col + 128] -= change[inside:, 128 * t : 128 * t + 128]
        if half == 0:
            change = product(1, (1, 2))
            for t, (ref, low, col) in enumerate(tiles[1:]):
                ref[128 + low : 256 + low, col : col + 128] -= change[:, 128 * t : 128 * t + 128]

    upper = row[:128, :128] <= lane[:128, :128]
    factor_ref[:128, :128] = jnp.where(upper, work[:128, :], 0.0)
    factor_ref[:128, 128:] = work[128:256, :]
    factor_ref[128:, :128] = jnp.zeros((128, 128), F32)
    factor_ref[128:, 128:] = jnp.where(upper, work[256:, :], 0.0)
    high, middle, _ = three_terms(inv[...])
    right = jnp.concatenate([high, middle, high], axis=1)
    place = place_ref[0]
    for shift, coeffs in enumerate((c0_ref, c1_ref, c2_ref, c3_ref)):
        first = pl.multiple_of(lax.rem(place + shift, 4) * PIECE, 16)
        high, middle, _ = three_terms(coeffs[...])
        left_side = jnp.concatenate([high, high, middle], axis=1)
        scores_ref[pl.ds(first, PIECE), :] = lax.dot_general(
            left_side, right, (((1,), (1,)), ((), ())), preferred_element_type=F32
        )


def factor_and_scores(place, core, halves, pieces):
    vmem = pl.BlockSpec(memory_space=pltpu.VMEM)
    return pl.pallas_call(
        factor_kernel,
        out_shape=(
            jax.ShapeDtypeStruct((PART, PROBES), F32),
            jax.ShapeDtypeStruct((PROBES, PROBES), F32),
        ),
        in_specs=[pl.BlockSpec(memory_space=pltpu.SMEM)] * 2 + [vmem] * 6,
        out_specs=(vmem, vmem),
        scratch_shapes=[pltpu.VMEM((2 * HALF, 128), F32), pltpu.VMEM((PROBES, PROBES), F32)],
        compiler_params=pltpu.CompilerParams(vmem_limit_bytes=12 * 1024 * 1024),
        name="factor",
    )(place, core, *halves, *pieces)


def shifted(value, shift):
    return lax.ppermute(value, "x", [(i, (i + shift) % 4) for i in range(4)])


def partner_of(step, z, y, core, x):
    if step < 4:
        flip = (1, 3)[step % 2]
        return (z, y, core, x ^ flip) if (step < 2) == (core == 0) else (z, y ^ flip, core, x)
    return (z ^ (1, 2, 6)[step - 4], y, core, x)


def exchanged(value, step):
    moves = []
    for z in range(8):
        for y in range(4):
            for core in range(2):
                for x in range(4):
                    to_z, to_y, to_core, to_x = partner_of(step, z, y, core, x)
                    source = ((z * 4 + y) * 2 + core) * 4 + x
                    moves.append((source, ((to_z * 4 + to_y) * 2 + to_core) * 4 + to_x))
    return lax.ppermute(value, ("z", "y", "core", "x"), moves)


def other_core(value):
    return lax.ppermute(value, "core", [(0, 1), (1, 0)])


def sum_everywhere(mine, other, coeffs):
    part = mine + other_core(other)
    for step in range(4):
        part = part + exchanged(part, step)
    pieces = []
    for step in range(4, 7):
        piece = shifted(coeffs, (2, 3, 1)[step - 4])
        part, piece = lax.optimization_barrier((part + exchanged(part, step), piece))
        pieces.append(piece)
    across, following, before = pieces
    return (part, other_core(part)), (following, across, before)


def body(images, panels, mean_panels, ctf_table, pose_bin, ctf_group):
    place = lax.axis_index("x").astype(jnp.int32).reshape(1)
    core = lax.axis_index("core").astype(jnp.int32).reshape(1)
    particles = PART * 64
    own, following, across, before = project(
        images, panels, mean_panels, ctf_table, pose_bin, ctf_group
    )
    across = shifted(across, 2)
    following = shifted(following, 1)
    before = shifted(before, 3)
    coeffs, mine, other = gram_of(core, (kept(own), following, across, before), particles)
    halves, pieces = sum_everywhere(mine, other, coeffs)
    return factor_and_scores(place, core, halves, (coeffs, *pieces))


def solution(mesh):
    fine = Mesh(mesh.devices.reshape(8, 4, 2, 4), ("z", "y", "core", "x"))
    dom = ("z", "y", "core")
    placed = (
        P(dom, "x"),
        P(dom, "x", None),
        P(dom, "x"),
        P(None, "x"),
        P(dom),
        P(dom),
    )
    return jax.shard_map(
        body, mesh=fine, in_specs=placed, out_specs=(P(dom, None), P()), check_vma=False
    )
```

```python
import functools

import jax
import jax.numpy as jnp
from jax import lax
from jax.experimental import pallas as pl
from jax.experimental.pallas import tpu as pltpu
from jax.sharding import Mesh, PartitionSpec as P

F32 = jnp.float32
BF16 = jnp.bfloat16
HIGHEST = lax.Precision.HIGHEST

PART = 448
PIECE = 112
PIX = 6400
CUTS = (0, 2048, 4352, 6400)
STEP = 1280
GROUPS = 16
PROBES = 256
HALF = 136


def three_terms(value):
    high = value.astype(BF16)
    rest = value - high.astype(F32)
    middle = rest.astype(BF16)
    low = (rest - middle.astype(F32)).astype(BF16)
    return high, middle, low


def project_kernel(
    pose_ref, group_ref, images_ref, panels_ref, mean_ref, ctf_ref,
    own_ref, next_ref, across_ref, before_ref,
    pose_in, group_in, images, panels, mean, ctf, weighted, total, picks, whole, sems, index_sems,
):
    chunks = [slice(first, last) for first, last in zip(CUTS[:-1], CUTS[1:])]
    copies = []
    for i, cut in enumerate(chunks):
        pairs = (
            (ctf_ref.at[:, cut], ctf.at[:, cut]),
            (mean_ref.at[:, cut], mean.at[:, cut]),
            (images_ref.at[:, cut], images.at[:, cut]),
            (panels_ref.at[0, cut, :], panels.at[0, cut, :]),
            (panels_ref.at[1, cut, :], panels.at[1, cut, :]),
        )
        copies.append([pltpu.make_async_copy(*pair, sems.at[i, j]) for j, pair in enumerate(pairs)])
    indices = (
        pltpu.make_async_copy(pose_ref, pose_in, index_sems.at[0]),
        pltpu.make_async_copy(group_ref, group_in, index_sems.at[1]),
    )
    for copy in (*indices, *copies[0]):
        copy.start()
    for copy in indices:
        copy.wait()

    rows = lax.broadcasted_iota(jnp.int32, (128, PART), 0)
    group = jnp.broadcast_to(group_in[...], (128, PART))
    pose = jnp.broadcast_to(pose_in[...], (128, PART))
    wanted = jnp.where(rows < 3 * GROUPS, lax.rem(rows, GROUPS), 1)
    found = jnp.where(rows < 3 * GROUPS, group, pose)
    picks[...] = jnp.where(wanted == found, 1.0, 0.0).astype(F32).T
    second = picks[:, 3 * GROUPS : 3 * GROUPS + 1] > 0.5
    chosen = picks[:, : 3 * GROUPS].astype(BF16)

    def weigh(cut):
        stack = jnp.concatenate(three_terms(ctf[:, cut]), axis=0)
        factor = jnp.dot(chosen, stack, preferred_element_type=F32)
        middle = jnp.where(second, mean[1:2, cut], mean[0:1, cut])
        weighted[:, cut] = (factor * (images[:, cut].astype(F32) - factor * middle)).astype(BF16)

    def add(cut):
        for which in range(2):
            part = jnp.dot(weighted[:, cut], panels[which, cut, :], preferred_element_type=F32)
            total[which] = part if cut.start == 0 else total[which] + part

    for i, chunk in enumerate(chunks):
        for copy in copies[i][:3]:
            copy.wait()
        if i + 1 < len(chunks):
            for copy in copies[i + 1]:
                copy.start()
        cuts = [slice(at, min(at + STEP, chunk.stop)) for at in range(chunk.start, chunk.stop, STEP)]
        weigh(cuts[0])
        for copy in copies[i][3:]:
            copy.wait()
        for j, cut in enumerate(cuts):
            if j + 1 < len(cuts):
                weigh(cuts[j + 1])
            add(cut)
    whole[...] = jnp.where(second, total[1], total[0])
    place = lax.axis_index("x")
    for shift, out in enumerate((own_ref, next_ref, across_ref, before_ref)):
        first = pl.multiple_of(lax.rem(place + shift, 4) * PIECE, 16)
        out[...] = whole[pl.ds(first, PIECE), :]


def project(images, panels, mean_panels, ctf_table, pose_bin, ctf_group):
    piece = jax.ShapeDtypeStruct((PIECE, PROBES), F32)
    vmem = pl.BlockSpec(memory_space=pltpu.VMEM)
    anywhere = pl.BlockSpec(memory_space=pl.ANY)
    return pl.pallas_call(
        project_kernel,
        out_shape=(piece,) * 4,
        in_specs=[anywhere] * 6,
        out_specs=(vmem,) * 4,
        scratch_shapes=[
            pltpu.VMEM((1, PART), jnp.int32),
            pltpu.VMEM((1, PART), jnp.int32),
            pltpu.VMEM((PART, PIX), BF16),
            pltpu.VMEM((2, PIX, PROBES), BF16),
            pltpu.VMEM((2, PIX), F32),
            pltpu.VMEM((GROUPS, PIX), F32),
            pltpu.VMEM((PART, PIX), BF16),
            pltpu.VMEM((2, PART, PROBES), F32),
            pltpu.VMEM((PART, 128), F32),
            pltpu.VMEM((PART, PROBES), F32),
            pltpu.SemaphoreType.DMA((len(CUTS) - 1, 5)),
            pltpu.SemaphoreType.DMA((2,)),
        ],
        compiler_params=pltpu.CompilerParams(vmem_limit_bytes=60 * 1024 * 1024),
        name="project",
    )(pose_bin.reshape(1, PART), ctf_group.reshape(1, PART), images, panels, mean_panels, ctf_table)


def keep_kernel(piece_ref, kept_ref):
    kept_ref[...] = piece_ref[...]


def kept(piece):
    vmem = pl.BlockSpec(memory_space=pltpu.VMEM)
    return pl.pallas_call(
        keep_kernel,
        out_shape=jax.ShapeDtypeStruct(piece.shape, piece.dtype),
        in_specs=[vmem],
        out_specs=vmem,
        compiler_params=pltpu.CompilerParams(vmem_limit_bytes=2 * 1024 * 1024),
        name="keep",
    )(piece)


def gram_kernel(core_ref, own_ref, first_ref, second_ref, third_ref, coeffs_ref, mine_ref, other_ref, packed, *, particles):
    coeffs = (own_ref[...] + first_ref[...]) + (second_ref[...] + third_ref[...])
    coeffs_ref[...] = coeffs

    def block(left, right):
        gram = lax.dot_general(
            left, right, (((0,), (0,)), ((), ())), precision=HIGHEST, preferred_element_type=F32
        )
        return gram / particles

    lane = lax.broadcasted_iota(jnp.int32, (128, 128), 1)
    row = lax.broadcasted_iota(jnp.int32, (128, 128), 0)
    top = block(coeffs[:, :128], coeffs)
    bottom = block(coeffs[:, 128:], coeffs[:, 128:])
    diagonal = jnp.sum(jnp.where(row == lane, bottom, 0.0), axis=0, keepdims=True)
    packed[:128, :] = top[:, 128:]
    packed[128:256, :] = jnp.where(row >= lane, top[:, :128], bottom)
    packed[256:, :] = jnp.broadcast_to(diagonal, (16, 128))
    core = core_ref[0]
    mine_ref[...] = packed[pl.ds(pl.multiple_of(core * HALF, 8), HALF), :]
    other_ref[...] = packed[pl.ds(pl.multiple_of((1 - core) * HALF, 8), HALF), :]


def gram_of(core, pieces, particles):
    vmem = pl.BlockSpec(memory_space=pltpu.VMEM)
    return pl.pallas_call(
        functools.partial(gram_kernel, particles=particles),
        out_shape=(
            jax.ShapeDtypeStruct((PIECE, PROBES), F32),
            jax.ShapeDtypeStruct((HALF, 128), F32),
            jax.ShapeDtypeStruct((HALF, 128), F32),
        ),
        in_specs=[pl.BlockSpec(memory_space=pltpu.SMEM)] + [vmem] * 4,
        out_specs=(vmem,) * 3,
        scratch_shapes=[pltpu.VMEM((2 * HALF, 128), F32)],
        compiler_params=pltpu.CompilerParams(vmem_limit_bytes=12 * 1024 * 1024),
        name="gram",
    )(core, *pieces)


def factor_kernel(
    place_ref, core_ref, mine_ref, other_ref, c0_ref, c1_ref, c2_ref, c3_ref, scores_ref, factor_ref, packed, work, inv
):
    lane = lax.broadcasted_iota(jnp.int32, (256, 256), 1)
    row = lax.broadcasted_iota(jnp.int32, (256, 256), 0)
    core = core_ref[0]
    packed[pl.ds(pl.multiple_of(core * HALF, 8), HALF), :] = mine_ref[...]
    packed[pl.ds(pl.multiple_of((1 - core) * HALF, 8), HALF), :] = other_ref[...]
    below = row[:128, :128] - lane[:128, :128]
    halves = packed[128:256, :]
    turned = halves.T
    work[:128, :] = jnp.where(below >= 0, halves, turned)
    work[128:256, :] = packed[:128, :]
    work[256:, :] = jnp.where(below < 0, halves, jnp.where(below > 0, turned, packed[256:257, :]))
    inv[...] = jnp.where(lane == row, 1.0, 0.0).astype(F32)
    sub = lax.broadcasted_iota(jnp.int32, (8, 128), 0)

    def spread(value):
        return jnp.broadcast_to(value, (8, 128))

    for block in range(8):
        start = 32 * block
        half = block // 4
        if half == 0:
            tiles = ((work, 0, 0), (work, 128, 0), (inv, 0, 0))
        else:
            tiles = ((work, 128, 0), (inv, 0, 0), (inv, 0, 128))
        rows = [
            [ref[start + low + 8 * g : start + low + 8 * g + 8, col : col + 128] for ref, low, col in tiles]
            for g in range(4)
        ]
        for g in range(4):
            at = start - 128 * half + 8 * g
            cols = [
                {h: spread(rows[h][0][:, at + k : at + k + 1]) for h in range(g, 4)} for k in range(8)
            ]
            pivots = jnp.ones((8, 128), F32)
            for k in range(8):
                heads = {j: spread(cols[j][g][k : k + 1, :]) for j in range(k, 8)}
                pivots = jnp.where(sub == k, heads[k], pivots)
                inverse = 1.0 / heads[k]
                ratio = {h: cols[k][h] * inverse for h in range(g, 4)}
                ratio[g] = jnp.where(sub > k, ratio[g], 0.0)
                for j in range(k + 1, 8):
                    for h in range(g, 4):
                        cols[j][h] = cols[j][h] - ratio[h] * heads[j]
                for t in range(3):
                    head = spread(rows[g][t][k : k + 1, :])
                    for h in range(g, 4):
                        rows[h][t] = rows[h][t] - ratio[h] * head
            scale = lax.rsqrt(pivots)
            rows[g] = [value * scale for value in rows[g]]
        done = [jnp.concatenate([rows[g][t] for g in range(4)], axis=0) for t in range(3)]
        for (ref, low, col), value in zip(tiles, done):
            ref[start + low : start + low + 32, col : col + 128] = value
        if block == 7:
            break
        terms = [three_terms(value) for value in done]

        def left(t):
            high, middle, low = terms[t]
            return jnp.concatenate([high, high, middle, high, middle, low], axis=0)

        def right(ts):
            high, middle, low = (jnp.concatenate([terms[t][i] for t in ts], axis=1) for i in range(3))
            return jnp.concatenate([high, middle, high, low, middle, high], axis=0)

        def product(t, ts):
            return lax.dot_general(
                left(t), right(ts), (((0,), (0,)), ((), ())), preferred_element_type=F32
            )

        inside = start - 128 * half + 32
        if inside < 128:
            change = product(0, (0, 1, 2))
            for t, (ref, low, col) in enumerate(tiles):
                last = 128 * half + 128 + low
                ref[start + 32 + low : last, col : col + 128] -= change[inside:, 128 * t : 128 * t + 128]
        if half == 0:
            change = product(1, (1, 2))
            for t, (ref, low, col) in enumerate(tiles[1:]):
                ref[128 + low : 256 + low, col : col + 128] -= change[:, 128 * t : 128 * t + 128]

    upper = row[:128, :128] <= lane[:128, :128]
    factor_ref[:128, :128] = jnp.where(upper, work[:128, :], 0.0)
    factor_ref[:128, 128:] = work[128:256, :]
    factor_ref[128:, :128] = jnp.zeros((128, 128), F32)
    factor_ref[128:, 128:] = jnp.where(upper, work[256:, :], 0.0)
    high, middle, _ = three_terms(inv[...])
    right = jnp.concatenate([high, middle, high], axis=1)
    place = place_ref[0]
    for shift, coeffs in enumerate((c0_ref, c1_ref, c2_ref, c3_ref)):
        first = pl.multiple_of(lax.rem(place + shift, 4) * PIECE, 16)
        high, middle, _ = three_terms(coeffs[...])
        left_side = jnp.concatenate([high, high, middle], axis=1)
        scores_ref[pl.ds(first, PIECE), :] = lax.dot_general(
            left_side, right, (((1,), (1,)), ((), ())), preferred_element_type=F32
        )


def factor_and_scores(place, core, halves, pieces):
    vmem = pl.BlockSpec(memory_space=pltpu.VMEM)
    return pl.pallas_call(
        factor_kernel,
        out_shape=(
            jax.ShapeDtypeStruct((PART, PROBES), F32),
            jax.ShapeDtypeStruct((PROBES, PROBES), F32),
        ),
        in_specs=[pl.BlockSpec(memory_space=pltpu.SMEM)] * 2 + [vmem] * 6,
        out_specs=(vmem, vmem),
        scratch_shapes=[
            pltpu.VMEM((2 * HALF, 128), F32),
            pltpu.VMEM((384, 128), F32),
            pltpu.VMEM((PROBES, PROBES), F32),
        ],
        compiler_params=pltpu.CompilerParams(vmem_limit_bytes=12 * 1024 * 1024),
        name="factor",
    )(place, core, *halves, *pieces)


def shifted(value, shift):
    return lax.ppermute(value, "x", [(i, (i + shift) % 4) for i in range(4)])


def partner_of(step, z, y, core, x):
    if step < 4:
        flip = (1, 3)[step % 2]
        return (z, y, core, x ^ flip) if (step < 2) == (core == 0) else (z, y ^ flip, core, x)
    return (z ^ (1, 2, 6)[step - 4], y, core, x)


def exchanged(value, step):
    moves = []
    for z in range(8):
        for y in range(4):
            for core in range(2):
                for x in range(4):
                    to_z, to_y, to_core, to_x = partner_of(step, z, y, core, x)
                    source = ((z * 4 + y) * 2 + core) * 4 + x
                    moves.append((source, ((to_z * 4 + to_y) * 2 + to_core) * 4 + to_x))
    return lax.ppermute(value, ("z", "y", "core", "x"), moves)


def other_core(value):
    return lax.ppermute(value, "core", [(0, 1), (1, 0)])


def sum_everywhere(mine, other, coeffs):
    part = mine + other_core(other)
    for step in range(4):
        part = part + exchanged(part, step)
    pieces = []
    for step in range(4, 7):
        piece = shifted(coeffs, (2, 3, 1)[step - 4])
        part, piece = lax.optimization_barrier((part + exchanged(part, step), piece))
        pieces.append(piece)
    across, following, before = pieces
    return (part, other_core(part)), (following, across, before)


def body(images, panels, mean_panels, ctf_table, pose_bin, ctf_group):
    place = lax.axis_index("x").astype(jnp.int32).reshape(1)
    core = lax.axis_index("core").astype(jnp.int32).reshape(1)
    particles = PART * 64
    own, following, across, before = project(
        images, panels, mean_panels, ctf_table, pose_bin, ctf_group
    )
    across = shifted(across, 2)
    following = shifted(following, 1)
    before = shifted(before, 3)
    coeffs, mine, other = gram_of(core, (kept(own), following, across, before), particles)
    halves, pieces = sum_everywhere(mine, other, coeffs)
    return factor_and_scores(place, core, halves, (coeffs, *pieces))


def solution(mesh):
    fine = Mesh(mesh.devices.reshape(8, 4, 2, 4), ("z", "y", "core", "x"))
    dom = ("z", "y", "core")
    placed = (
        P(dom, "x"),
        P(dom, "x", None),
        P(dom, "x"),
        P(None, "x"),
        P(dom),
        P(dom),
    )
    return jax.shard_map(
        body, mesh=fine, in_specs=placed, out_specs=(P(dom, None), P()), check_vma=False
    )
```

```python
import functools

import jax
import jax.numpy as jnp
from jax import lax
from jax.experimental import pallas as pl
from jax.experimental.pallas import tpu as pltpu
from jax.sharding import Mesh, PartitionSpec as P

F32 = jnp.float32
BF16 = jnp.bfloat16
HIGHEST = lax.Precision.HIGHEST

PART = 448
PIECE = 112
PIX = 6400
CUTS = (0, 2048, 4352, 6400)
STEP = 1280
GROUPS = 16
PROBES = 256
HALF = 136


def three_terms(value):
    high = value.astype(BF16)
    rest = value - high.astype(F32)
    middle = rest.astype(BF16)
    low = (rest - middle.astype(F32)).astype(BF16)
    return high, middle, low


def project_kernel(
    pose_ref, group_ref, images_ref, panels_ref, mean_ref, ctf_ref,
    own_ref, next_ref, across_ref, before_ref,
    pose_in, group_in, images, panels, mean, ctf, weighted, total, picks, whole, sems, index_sems,
):
    chunks = [slice(first, last) for first, last in zip(CUTS[:-1], CUTS[1:])]
    copies = []
    for i, cut in enumerate(chunks):
        pairs = (
            (ctf_ref.at[:, cut], ctf.at[:, cut]),
            (mean_ref.at[:, cut], mean.at[:, cut]),
            (images_ref.at[:, cut], images.at[:, cut]),
            (panels_ref.at[0, cut, :], panels.at[0, cut, :]),
            (panels_ref.at[1, cut, :], panels.at[1, cut, :]),
        )
        copies.append([pltpu.make_async_copy(*pair, sems.at[i, j]) for j, pair in enumerate(pairs)])
    indices = (
        pltpu.make_async_copy(pose_ref, pose_in, index_sems.at[0]),
        pltpu.make_async_copy(group_ref, group_in, index_sems.at[1]),
    )
    for copy in (*indices, *copies[0]):
        copy.start()
    for copy in indices:
        copy.wait()

    rows = lax.broadcasted_iota(jnp.int32, (128, PART), 0)
    group = jnp.broadcast_to(group_in[...], (128, PART))
    pose = jnp.broadcast_to(pose_in[...], (128, PART))
    wanted = jnp.where(rows < 3 * GROUPS, lax.rem(rows, GROUPS), 1)
    found = jnp.where(rows < 3 * GROUPS, group, pose)
    picks[...] = jnp.where(wanted == found, 1.0, 0.0).astype(F32).T
    second = picks[:, 3 * GROUPS : 3 * GROUPS + 1] > 0.5
    chosen = picks[:, : 3 * GROUPS].astype(BF16)

    def weigh(cut):
        stack = jnp.concatenate(three_terms(ctf[:, cut]), axis=0)
        factor = jnp.dot(chosen, stack, preferred_element_type=F32)
        middle = jnp.where(second, mean[1:2, cut], mean[0:1, cut])
        weighted[:, cut] = (factor * (images[:, cut].astype(F32) - factor * middle)).astype(BF16)

    def add(cut):
        for which in range(2):
            part = jnp.dot(weighted[:, cut], panels[which, cut, :], preferred_element_type=F32)
            total[which] = part if cut.start == 0 else total[which] + part

    for i, chunk in enumerate(chunks):
        for copy in copies[i][:3]:
            copy.wait()
        if i + 1 < len(chunks):
            for copy in copies[i + 1]:
                copy.start()
        cuts = [slice(at, min(at + STEP, chunk.stop)) for at in range(chunk.start, chunk.stop, STEP)]
        weigh(cuts[0])
        for copy in copies[i][3:]:
            copy.wait()
        for j, cut in enumerate(cuts):
            if j + 1 < len(cuts):
                weigh(cuts[j + 1])
            add(cut)
    whole[...] = jnp.where(second, total[1], total[0])
    place = lax.axis_index("x")
    for shift, out in enumerate((own_ref, next_ref, across_ref, before_ref)):
        first = pl.multiple_of(lax.rem(place + shift, 4) * PIECE, 16)
        out[...] = whole[pl.ds(first, PIECE), :]


def project(images, panels, mean_panels, ctf_table, pose_bin, ctf_group):
    piece = jax.ShapeDtypeStruct((PIECE, PROBES), F32)
    vmem = pl.BlockSpec(memory_space=pltpu.VMEM)
    anywhere = pl.BlockSpec(memory_space=pl.ANY)
    return pl.pallas_call(
        project_kernel,
        out_shape=(piece,) * 4,
        in_specs=[anywhere] * 6,
        out_specs=(vmem,) * 4,
        scratch_shapes=[
            pltpu.VMEM((1, PART), jnp.int32),
            pltpu.VMEM((1, PART), jnp.int32),
            pltpu.VMEM((PART, PIX), BF16),
            pltpu.VMEM((2, PIX, PROBES), BF16),
            pltpu.VMEM((2, PIX), F32),
            pltpu.VMEM((GROUPS, PIX), F32),
            pltpu.VMEM((PART, PIX), BF16),
            pltpu.VMEM((2, PART, PROBES), F32),
            pltpu.VMEM((PART, 128), F32),
            pltpu.VMEM((PART, PROBES), F32),
            pltpu.SemaphoreType.DMA((len(CUTS) - 1, 5)),
            pltpu.SemaphoreType.DMA((2,)),
        ],
        compiler_params=pltpu.CompilerParams(vmem_limit_bytes=60 * 1024 * 1024),
        name="project",
    )(pose_bin.reshape(1, PART), ctf_group.reshape(1, PART), images, panels, mean_panels, ctf_table)


def keep_kernel(piece_ref, kept_ref):
    kept_ref[...] = piece_ref[...]


def kept(piece):
    vmem = pl.BlockSpec(memory_space=pltpu.VMEM)
    return pl.pallas_call(
        keep_kernel,
        out_shape=jax.ShapeDtypeStruct(piece.shape, piece.dtype),
        in_specs=[vmem],
        out_specs=vmem,
        compiler_params=pltpu.CompilerParams(vmem_limit_bytes=2 * 1024 * 1024),
        name="keep",
    )(piece)


def gram_kernel(core_ref, own_ref, first_ref, second_ref, third_ref, coeffs_ref, mine_ref, other_ref, packed, *, particles):
    coeffs = (own_ref[...] + first_ref[...]) + (second_ref[...] + third_ref[...])
    coeffs_ref[...] = coeffs

    def block(left, right):
        gram = lax.dot_general(
            left, right, (((0,), (0,)), ((), ())), precision=HIGHEST, preferred_element_type=F32
        )
        return gram / particles

    lane = lax.broadcasted_iota(jnp.int32, (128, 128), 1)
    row = lax.broadcasted_iota(jnp.int32, (128, 128), 0)
    top = block(coeffs[:, :128], coeffs)
    bottom = block(coeffs[:, 128:], coeffs[:, 128:])
    diagonal = jnp.sum(jnp.where(row == lane, bottom, 0.0), axis=0, keepdims=True)
    packed[:128, :] = top[:, 128:]
    packed[128:256, :] = jnp.where(row >= lane, top[:, :128], bottom)
    packed[256:, :] = jnp.broadcast_to(diagonal, (16, 128))
    core = core_ref[0]
    mine_ref[...] = packed[pl.ds(pl.multiple_of(core * HALF, 8), HALF), :]
    other_ref[...] = packed[pl.ds(pl.multiple_of((1 - core) * HALF, 8), HALF), :]


def gram_of(core, pieces, particles):
    vmem = pl.BlockSpec(memory_space=pltpu.VMEM)
    return pl.pallas_call(
        functools.partial(gram_kernel, particles=particles),
        out_shape=(
            jax.ShapeDtypeStruct((PIECE, PROBES), F32),
            jax.ShapeDtypeStruct((HALF, 128), F32),
            jax.ShapeDtypeStruct((HALF, 128), F32),
        ),
        in_specs=[pl.BlockSpec(memory_space=pltpu.SMEM)] + [vmem] * 4,
        out_specs=(vmem,) * 3,
        scratch_shapes=[pltpu.VMEM((2 * HALF, 128), F32)],
        compiler_params=pltpu.CompilerParams(vmem_limit_bytes=12 * 1024 * 1024),
        name="gram",
    )(core, *pieces)


def factor_kernel(
    core_ref, mine_ref, other_ref, c0_ref, c1_ref, c2_ref, c3_ref, scores_ref, factor_ref,
    packed, work, inv, whole, made, sems,
):
    lane = lax.broadcasted_iota(jnp.int32, (256, 256), 1)
    row = lax.broadcasted_iota(jnp.int32, (256, 256), 0)
    core = core_ref[0]
    packed[pl.ds(pl.multiple_of(core * HALF, 8), HALF), :] = mine_ref[...]
    packed[pl.ds(pl.multiple_of((1 - core) * HALF, 8), HALF), :] = other_ref[...]
    below = row[:128, :128] - lane[:128, :128]
    halves = packed[128:256, :]
    turned = halves.T
    work[:128, :] = jnp.where(below >= 0, halves, turned)
    work[128:256, :] = packed[:128, :]
    work[256:, :] = jnp.where(below < 0, halves, jnp.where(below > 0, turned, packed[256:257, :]))
    inv[...] = jnp.where(lane == row, 1.0, 0.0).astype(F32)
    sub = lax.broadcasted_iota(jnp.int32, (8, 128), 0)

    def spread(value):
        return jnp.broadcast_to(value, (8, 128))

    for block in range(8):
        start = 32 * block
        half = block // 4
        if half == 0:
            tiles = ((work, 0, 0), (work, 128, 0), (inv, 0, 0))
        else:
            tiles = ((work, 128, 0), (inv, 0, 0), (inv, 0, 128))
        rows = [
            [ref[start + low + 8 * g : start + low + 8 * g + 8, col : col + 128] for ref, low, col in tiles]
            for g in range(4)
        ]
        for g in range(4):
            at = start - 128 * half + 8 * g
            cols = [
                {h: spread(rows[h][0][:, at + k : at + k + 1]) for h in range(g, 4)} for k in range(8)
            ]
            pivots = jnp.ones((8, 128), F32)
            for k in range(8):
                heads = {j: spread(cols[j][g][k : k + 1, :]) for j in range(k, 8)}
                pivots = jnp.where(sub == k, heads[k], pivots)
                inverse = 1.0 / heads[k]
                ratio = {h: cols[k][h] * inverse for h in range(g, 4)}
                ratio[g] = jnp.where(sub > k, ratio[g], 0.0)
                for j in range(k + 1, 8):
                    for h in range(g, 4):
                        cols[j][h] = cols[j][h] - ratio[h] * heads[j]
                for t in range(3):
                    head = spread(rows[g][t][k : k + 1, :])
                    for h in range(g, 4):
                        rows[h][t] = rows[h][t] - ratio[h] * head
            scale = lax.rsqrt(pivots)
            rows[g] = [value * scale for value in rows[g]]
        done = [jnp.concatenate([rows[g][t] for g in range(4)], axis=0) for t in range(3)]
        for (ref, low, col), value in zip(tiles, done):
            ref[start + low : start + low + 32, col : col + 128] = value
        if block == 7:
            break
        terms = [three_terms(value) for value in done]

        def left(t):
            high, middle, low = terms[t]
            return jnp.concatenate([high, high, middle, high, middle, low], axis=0)

        def right(ts):
            high, middle, low = (jnp.concatenate([terms[t][i] for t in ts], axis=1) for i in range(3))
            return jnp.concatenate([high, middle, high, low, middle, high], axis=0)

        def product(t, ts):
            return lax.dot_general(
                left(t), right(ts), (((0,), (0,)), ((), ())), preferred_element_type=F32
            )

        inside = start - 128 * half + 32
        if inside < 128:
            change = product(0, (0, 1, 2))
            for t, (ref, low, col) in enumerate(tiles):
                last = 128 * half + 128 + low
                ref[start + 32 + low : last, col : col + 128] -= change[inside:, 128 * t : 128 * t + 128]
        if half == 0:
            change = product(1, (1, 2))
            for t, (ref, low, col) in enumerate(tiles[1:]):
                ref[128 + low : 256 + low, col : col + 128] -= change[:, 128 * t : 128 * t + 128]

    upper = row[:128, :128] <= lane[:128, :128]
    whole[:128, :128] = jnp.where(upper, work[:128, :], 0.0)
    whole[:128, 128:] = work[128:256, :]
    whole[128:, :128] = jnp.zeros((128, 128), F32)
    whole[128:, 128:] = jnp.where(upper, work[256:, :], 0.0)
    copies = [pltpu.make_async_copy(whole, factor_ref, sems.at[4])]
    copies[0].start()
    high, middle, _ = three_terms(inv[...])
    right = jnp.concatenate([high, middle, high], axis=1)
    place = lax.axis_index("x")
    for shift, coeffs in enumerate((c0_ref, c1_ref, c2_ref, c3_ref)):
        high, middle, _ = three_terms(coeffs[...])
        left_side = jnp.concatenate([high, high, middle], axis=1)
        made[shift] = lax.dot_general(
            left_side, right, (((1,), (1,)), ((), ())), preferred_element_type=F32
        )
        first = pl.multiple_of(lax.rem(place + shift, 4) * PIECE, 16)
        copies.append(
            pltpu.make_async_copy(made.at[shift], scores_ref.at[pl.ds(first, PIECE), :], sems.at[shift])
        )
        copies[-1].start()
    for copy in copies:
        copy.wait()


def factor_and_scores(core, halves, pieces):
    vmem = pl.BlockSpec(memory_space=pltpu.VMEM)
    return pl.pallas_call(
        factor_kernel,
        out_shape=(
            jax.ShapeDtypeStruct((PART, PROBES), F32),
            jax.ShapeDtypeStruct((PROBES, PROBES), F32),
        ),
        in_specs=[pl.BlockSpec(memory_space=pltpu.SMEM)] + [vmem] * 6,
        out_specs=(pl.BlockSpec(memory_space=pl.ANY),) * 2,
        scratch_shapes=[
            pltpu.VMEM((2 * HALF, 128), F32),
            pltpu.VMEM((384, 128), F32),
            pltpu.VMEM((PROBES, PROBES), F32),
            pltpu.VMEM((PROBES, PROBES), F32),
            pltpu.VMEM((4, PIECE, PROBES), F32),
            pltpu.SemaphoreType.DMA((5,)),
        ],
        compiler_params=pltpu.CompilerParams(vmem_limit_bytes=12 * 1024 * 1024),
        name="factor",
    )(core, *halves, *pieces)


def shifted(value, shift):
    return lax.ppermute(value, "x", [(i, (i + shift) % 4) for i in range(4)])


def partner_of(step, z, y, core, x):
    if step < 4:
        flip = (1, 3)[step % 2]
        return (z, y, core, x ^ flip) if (step < 2) == (core == 0) else (z, y ^ flip, core, x)
    return (z ^ (1, 2, 6)[step - 4], y, core, x)


def exchanged(value, step):
    moves = []
    for z in range(8):
        for y in range(4):
            for core in range(2):
                for x in range(4):
                    to_z, to_y, to_core, to_x = partner_of(step, z, y, core, x)
                    source = ((z * 4 + y) * 2 + core) * 4 + x
                    moves.append((source, ((to_z * 4 + to_y) * 2 + to_core) * 4 + to_x))
    return lax.ppermute(value, ("z", "y", "core", "x"), moves)


def other_core(value):
    return lax.ppermute(value, "core", [(0, 1), (1, 0)])


def sum_everywhere(mine, other, coeffs):
    part = mine + other_core(other)
    for step in range(4):
        part = part + exchanged(part, step)
    pieces = []
    for step in range(4, 7):
        piece = shifted(coeffs, (2, 3, 1)[step - 4])
        part, piece = lax.optimization_barrier((part + exchanged(part, step), piece))
        pieces.append(piece)
    across, following, before = pieces
    return (part, other_core(part)), (following, across, before)


def body(images, panels, mean_panels, ctf_table, pose_bin, ctf_group):
    core = lax.axis_index("core").astype(jnp.int32).reshape(1)
    particles = PART * 64
    own, following, across, before = project(
        images, panels, mean_panels, ctf_table, pose_bin, ctf_group
    )
    across = shifted(across, 2)
    following = shifted(following, 1)
    before = shifted(before, 3)
    coeffs, mine, other = gram_of(core, (kept(own), following, across, before), particles)
    halves, pieces = sum_everywhere(mine, other, coeffs)
    return factor_and_scores(core, halves, (coeffs, *pieces))


def solution(mesh):
    fine = Mesh(mesh.devices.reshape(8, 4, 2, 4), ("z", "y", "core", "x"))
    dom = ("z", "y", "core")
    placed = (
        P(dom, "x"),
        P(dom, "x", None),
        P(dom, "x"),
        P(None, "x"),
        P(dom),
        P(dom),
    )
    return jax.shard_map(
        body, mesh=fine, in_specs=placed, out_specs=(P(dom, None), P()), check_vma=False
    )
```
